128 devices in a mesh: req: 8 (over x, y_lo), ctx: 16 (over y_hi, z, core).
Axes of the slice: x: 4, y: 4 (y_hi: 2, y_lo: 2; y = y_hi * 2 + y_lo), z: 4, core: 2. Of those that a mesh axis runs over, the one named last changes fastest.
Arguments:
- cand_feats: bfloat16 [65536, 512], P(('req', 'ctx')), may hold values from -6 to 6
- cand_user: int32 [65536, 1], P(('req', 'ctx')), may hold values from 0 to 7; in each aligned block of 512 rows (0 to 511, 512 to 1023, ...) at most 96 rows name the same one
- history: bfloat16 [8, 2048, 512], P('req', 'ctx'), may hold values from -6 to 6
- hist_len: int32 [8], replicated, may hold values from 128 to 2048, as said below
- hist_bucket: int32 [8, 2048], P('req', 'ctx'), may hold values from 0 to 127
- w_qu: bfloat16 [2, 512, 1024], replicated, may hold values from -0.625 to 0.625
- w_kv: bfloat16 [2, 512, 1024], replicated, may hold values from -0.625 to 0.625
- w_out: bfloat16 [2, 512, 512], replicated, may hold values from -0.25 to 0.25
- bias_table: float32 [2, 8, 128], replicated, may hold values from -9 to -4
- mlp_in: bfloat16 [512, 1024], replicated, may hold values from -0.25 to 0.25
- mlp_out: bfloat16 [1024, 8], replicated, may hold values from -0.1875 to 0.1875
Outputs:
- encoded: bfloat16 [65536, 512], P(('req', 'ctx'))
- task_logits: float32 [65536, 8], P(('req', 'ctx'))
The draws below stay inside these ranges and needn't reach their ends.
Inputs may be any that keep to these rules, and one draw needn't show every extreme that they name: `cand_user`: in each aligned block of 512 rows (the rows of one device) no user is named by more than 96 rows; in every draw some block names some user exactly 96 times. Events at positions hist_len[u] and later are not part of user u's history; in every draw some user has all 2048 events.
All inputs are finite; a program needn't handle non-finite values.
Results may differ from the reference program's by a relative error of at most 0.015.
Values may be sent and summed in bfloat16 or wider, within the bound.
No kernel may reach another device: no remote copies, remote signals or barrier semaphores. Data moves between devices by JAX's collectives and lax.ppermute only.
A program may use at most 128 MiB of HBM per device.

```python
import math
import jax
import jax.numpy as jnp
import numpy as np
from jax import lax

D = 512
HEADS = 8
HEAD_DIM = 64
LAYERS = 2
BUCKETS = 128
MLP_H = 1024
TASKS = 8
REQ_DEV = 512
USERS = 8
CAP = 96
HIST = 2048
REQ_ROWS = 65536


def draw_hist_len(key, part):
    key = jax.random.fold_in(key, 7)
    key_scale, key_trim, key_full = jax.random.split(key, 3)
    halving = jax.random.randint(key_scale, (USERS,), 0, 4)
    ceiling = jnp.right_shift(jnp.full((USERS,), HIST, jnp.int32), halving.astype(jnp.int32))
    trimmed = jax.random.randint(key_trim, (USERS,), 0, ceiling // 2 + 1)
    lengths = ceiling - trimmed
    longest = jax.random.randint(key_full, (), 0, USERS)
    return jnp.where(jnp.arange(USERS) == longest, HIST, lengths).astype(jnp.int32)


def place_ends(entries, key, least, high):
    shape = entries.shape
    place = [jax.random.randint(jax.random.fold_in(key, axis), (), 0, shape[axis]) for axis in range(len(shape))]
    entries = entries.at[tuple(place)].set(least)
    longest = shape.index(max(shape))
    place[longest] = (place[longest] + 1) % shape[longest]
    return entries.at[tuple(place)].set(high)


def level_of(own_key, extent, cuts, low, high):
    def one(dim, parts):
        draws = jax.random.uniform(jax.random.fold_in(jax.random.fold_in(own_key, 6), dim), (parts,), jnp.float32, low / len(cuts), high / len(cuts))
        return jnp.repeat(jnp.exp(draws), extent[dim] // parts).reshape((-1,) + (1,) * (len(extent) - dim - 1))

    loudness = one(*cuts[0])
    for cut in cuts[1:]:
        loudness = loudness * one(*cut)
    return loudness


def assign_block(stream_key, own, number, rows, number_of, top, most, lean):
    order = jax.random.permutation(stream_key, number_of)
    crowded, usual = shares(number_of, rows * top, most, lean, True), shares(number_of, rows * top, most, lean, False)
    places = jnp.arange(number_of)

    def named(sizes, turn):
        used = int((sizes > 0).sum())
        fixed = max(1, used // 4)
        passed = fixed + (places - fixed + turn * (used - fixed)) % max(1, number_of - fixed)
        return jnp.zeros((number_of,), jnp.int32).at[order[jnp.where(places < fixed, places, passed)]].set(jnp.asarray(sizes, jnp.int32))

    sizes = jnp.where(number % 4 == 0, named(crowded, number // 4), named(usual, number - number // 4 - 1))
    mixed = jax.random.permutation(jax.random.fold_in(own, 3), number_of)
    giver, taker = mixed[0:number_of // 2 * 2:2], mixed[1:number_of // 2 * 2:2]
    margin = jnp.minimum(sizes[giver] - 1, most - sizes[taker]) // 2
    margin = jnp.where((giver == order[0]) | (taker == order[0]) | (sizes[taker] == 0), 0, jnp.maximum(margin, 0))
    passed = jax.random.randint(jax.random.fold_in(own, 4), (number_of // 2,), 0, 1 << 20) % (margin + 1)
    sizes = sizes.at[giver].add(-passed).at[taker].add(passed)
    labels = jnp.searchsorted(jnp.cumsum(sizes), jnp.arange(rows * top), side="right").astype(jnp.int32)
    table = labels.reshape(top, rows).T
    table = table[jax.random.permutation(jax.random.fold_in(own, 1), rows)]
    turn = jax.random.randint(jax.random.fold_in(own, 2), (rows, 1), 0, top)
    return jnp.take_along_axis(table, (jnp.arange(top)[None, :] + turn) % top, axis=1)


def shares(count, total, most, lean, full):
    portions = [(1 << 20) // math.isqrt(grade ** lean) + 1 for grade in range(1, count + 1)]
    largest = most if full else min(most, max(-(-total // count), total * portions[0] // sum(portions)))
    least = 1 if total - largest >= count - 1 else 0
    holding, surplus = [largest] + [least] * (count - 1), total - largest - least * (count - 1)
    while surplus > 0:
        movable = [i for i in range(1, count) if holding[i] < largest] or [i for i in range(1, count) if holding[i] < most]
        pool, budget = sum([portions[i] for i in movable]), surplus
        for i in movable:
            addition = min(most - holding[i], max(1, budget * portions[i] // pool), surplus)
            holding[i] = holding[i] + addition
            surplus = surplus - addition
    return np.array(holding)


def centred(own_key, extent, scale, reach, cuts=(), held_as=jnp.bfloat16):
    values = scale * jax.random.normal(own_key, extent, jnp.float32)
    if cuts:
        values = values * level_of(own_key, extent, cuts, -0.22, 0.18)
    return jnp.clip(values, -reach, reach).astype(held_as)


def setup_inputs(seed: int = 0) -> dict:
    key_of = jax.random.split(jax.random.key(seed), 12)
    cand_feats = centred(key_of[0], (REQ_ROWS, D), 1.0, 6.0, ((0, 128),))
    cand_user_keys = jax.random.split(jax.random.fold_in(key_of[1], 1), REQ_ROWS // REQ_DEV)
    cand_user_turns = jax.random.permutation(jax.random.fold_in(key_of[1], 3), REQ_ROWS // REQ_DEV)
    cand_user = jax.vmap(lambda own, number: assign_block(jax.random.fold_in(key_of[1], 2), own, number, REQ_DEV, USERS, 1, CAP, 1))(cand_user_keys, cand_user_turns).reshape((REQ_ROWS, 1))
    history = centred(key_of[2], (USERS, HIST, D), 1.0, 6.0, ((0, 8), (1, 16)))
    hist_len = draw_hist_len(jax.random.fold_in(key_of[11], 71), 0)
    hist_bucket = place_ends(jax.random.randint(key_of[4], (USERS, HIST), 0, BUCKETS), jax.random.fold_in(key_of[4], 1), 0, BUCKETS - 1).astype(jnp.int32)
    w_qu = centred(key_of[5], (LAYERS, D, 2 * D), (4 * D // 25) ** -0.5, 0.625)
    w_kv = centred(key_of[6], (LAYERS, D, 2 * D), (4 * D // 25) ** -0.5, 0.625)
    w_out = centred(key_of[7], (LAYERS, D, D), D ** -0.5, 0.25)
    bias_table = jnp.clip(jax.random.uniform(key_of[8], (LAYERS, HEADS, BUCKETS), jnp.float32, -9.0, -4.0), -9.0, -4.0)
    mlp_in = centred(key_of[9], (D, MLP_H), D ** -0.5, 0.25)
    mlp_out = centred(key_of[10], (MLP_H, TASKS), MLP_H ** -0.5, 0.1875)
    return dict(cand_feats=cand_feats, cand_user=cand_user, history=history, hist_len=hist_len, hist_bucket=hist_bucket, w_qu=w_qu, w_kv=w_kv, w_out=w_out, bias_table=bias_table, mlp_in=mlp_in, mlp_out=mlp_out)


def layer_norm(values):
    average = lax.optimization_barrier(jnp.mean(values, axis=-1, keepdims=True))
    centered = values - average
    spread = lax.optimization_barrier(jnp.mean(centered * centered, axis=-1, keepdims=True))
    return centered * lax.rsqrt(spread + 1e-05)

def attend_block(queries, key_rows, value_rows, key_bias, first_row, hist_length):
    slot_count = queries.shape[0]
    query_heads = queries.astype(jnp.float32).reshape(slot_count, HEADS, HEAD_DIM)
    key_heads = key_rows.astype(jnp.float32).reshape(-1, HEADS, HEAD_DIM)
    value_heads = value_rows.astype(jnp.float32).reshape(-1, HEADS, HEAD_DIM)
    scores = jnp.einsum('shd,rhd->hsr', query_heads, key_heads) * HEAD_DIM ** (-0.5)
    scores = scores + key_bias.astype(jnp.float32).T[:, None, :]
    position = first_row + jnp.arange(key_rows.shape[0], dtype=jnp.int32)
    live_keys = position < hist_length
    weights = jnp.where(live_keys[None, None, :], jax.nn.silu(scores), 0.0).astype(jnp.bfloat16)
    mixed = jnp.einsum('hsr,rhd->shd', weights.astype(jnp.float32), value_heads)
    return mixed.reshape(slot_count, HEADS * HEAD_DIM)

def all_keys(queries, cache_layer, hist_length):
    key_rows, value_rows, key_bias = cache_layer
    block_rows = min(512, HIST)

    def step_fn(block_index, running):
        offset = (block_index * block_rows).astype(jnp.int32)
        key_part = lax.dynamic_slice_in_dim(key_rows, offset, block_rows, 0)
        value_part = lax.dynamic_slice_in_dim(value_rows, offset, block_rows, 0)
        bias_part = lax.dynamic_slice_in_dim(key_bias, offset, block_rows, 0)
        return running + attend_block(queries, key_part, value_part, bias_part, offset, hist_length)
    start_sum = jnp.zeros((queries.shape[0], D), jnp.float32)
    return lax.fori_loop(0, HIST // block_rows, step_fn, start_sum)

def user_cache(rows, buckets, w_kv, bias_table):
    normed = layer_norm(rows.astype(jnp.float32)).astype(jnp.bfloat16)
    cache = []
    for layer_index in range(LAYERS):
        projected = jax.nn.silu(jnp.dot(normed, w_kv[layer_index], preferred_element_type=jnp.float32)).astype(jnp.bfloat16)
        key_bias = bias_table[layer_index][:, buckets].T.astype(jnp.bfloat16)
        cache.append((projected[:, :D], projected[:, D:], key_bias))
    return cache

def run_layers(rows_in, cache, hist_length, w_qu, w_out):
    current = rows_in.astype(jnp.float32)
    for layer_index in range(LAYERS):
        normed = layer_norm(current).astype(jnp.bfloat16)
        projected = jax.nn.silu(jnp.dot(normed, w_qu[layer_index], preferred_element_type=jnp.float32))
        queries = projected[:, :D].astype(jnp.bfloat16)
        gate_part = projected[:, D:]
        mixed = all_keys(queries, cache[layer_index], hist_length)
        shaped = (layer_norm(mixed) * gate_part).astype(jnp.bfloat16)
        current = current + jnp.dot(shaped, w_out[layer_index], preferred_element_type=jnp.float32)
    return current.astype(jnp.bfloat16)

def reference(cand_feats, cand_user, history, hist_len, hist_bucket, w_qu, w_kv, w_out, bias_table, mlp_in, mlp_out):
    owners = cand_user[:, 0].astype(jnp.int32)
    row_total = owners.shape[0]
    block_rows = 512
    order = jnp.argsort(owners, stable=True).astype(jnp.int32)
    ordered = jnp.concatenate([cand_feats[order], jnp.zeros((block_rows, D), jnp.bfloat16)], 0)
    members = (owners[:, None] == jnp.arange(USERS, dtype=jnp.int32)[None, :]).astype(jnp.int32)
    counts = lax.optimization_barrier(jnp.sum(members, axis=0)).astype(jnp.int32)
    starts = (jnp.cumsum(counts).astype(jnp.int32) - counts).astype(jnp.int32)
    result = jnp.zeros((row_total + block_rows, D), jnp.bfloat16)

    def per_user(user_index, result):
        cache = user_cache(history[user_index], hist_bucket[user_index], w_kv, bias_table)
        hist_length = hist_len[user_index]

        def per_block(block_index, result):
            offset = (starts[user_index] + block_index * block_rows).astype(jnp.int32)
            rows_in = lax.dynamic_slice_in_dim(ordered, offset, block_rows, 0)
            finished = run_layers(rows_in, cache, hist_length, w_qu, w_out)
            return lax.dynamic_update_slice_in_dim(result, finished, offset, 0)
        block_total = ((counts[user_index] + block_rows - 1) // block_rows).astype(jnp.int32)
        return lax.fori_loop(0, block_total, per_block, result)
    result = lax.fori_loop(0, USERS, per_user, result)
    encoded = jnp.zeros((row_total, D), jnp.bfloat16).at[order].set(result[:row_total])
    normed_out = layer_norm(encoded.astype(jnp.float32)).astype(jnp.bfloat16)
    mlp_hidden = jax.nn.silu(jnp.dot(normed_out, mlp_in, preferred_element_type=jnp.float32)).astype(jnp.bfloat16)
    task_logits = jnp.dot(mlp_hidden, mlp_out, preferred_element_type=jnp.float32)
    return (encoded, task_logits)
```

```python
import functools

import jax
import jax.numpy as jnp
from jax import lax
from jax.experimental import pallas as pl
from jax.experimental.pallas import tpu as pltpu
from jax.sharding import PartitionSpec as P

BF16 = jnp.bfloat16
F32 = jnp.float32
NT = (((1,), (1,)), ((), ()))
TN = (((0,), (0,)), ((), ()))
TT = (((0,), (1,)), ((), ()))
MIB = 2**20
BIAS_ROWS = 16


def dot(left, right, dims=(((1,), (0,)), ((), ()))):
    return lax.dot_general(left, right, dims, preferred_element_type=F32)


def layer_norm(values):
    average = jnp.mean(values, axis=-1, keepdims=True)
    centered = values - average
    spread = jnp.mean(centered * centered, axis=-1, keepdims=True)
    return centered * lax.rsqrt(spread + 1e-05)


def silu_of_half(half):
    return half + half * jnp.tanh(half)


def silu(values):
    return silu_of_half(0.5 * values)


def slots_of(owner_column, groups, capacity):
    rows = owner_column.shape[0]
    members = owner_column == lax.broadcasted_iota(jnp.int32, (rows, groups), 1)
    before = lax.broadcasted_iota(jnp.int32, (rows, rows), 1) < lax.broadcasted_iota(
        jnp.int32, (rows, rows), 0
    )
    earlier = dot(before.astype(BF16), members.astype(BF16))
    base = lax.broadcasted_iota(jnp.int32, (rows, groups), 1).astype(F32) * capacity
    slot = jnp.sum(jnp.where(members, earlier + base, 0.0), axis=1, keepdims=True)
    return slot.astype(jnp.int32)


def dispatch_kernel(groups, capacity, len_ref, feats_ref, owner_ref, hist_ref, bucket_ref, table_ref, out_ref, keys_ref):
    rows = feats_ref.shape[0]
    slot_count = groups * capacity
    slot = slots_of(owner_ref[...], groups, capacity)
    place = (slot == lax.broadcasted_iota(jnp.int32, (rows, slot_count), 1)).astype(BF16)
    out_ref[...] = dot(place, feats_ref[...], TN).astype(BF16)
    key_count = hist_ref.shape[0]
    live = len_ref[lax.axis_index("req")] - lax.axis_index("ctx") * key_count
    normed = layer_norm(hist_ref[...].astype(F32))
    position = lax.broadcasted_iota(jnp.int32, normed.shape, 0)
    keys_ref[:key_count, :] = jnp.where(position < live, normed, 0.0).astype(BF16)
    bucket_count = table_ref.shape[1]
    onehot = lax.broadcasted_iota(jnp.int32, (bucket_count, key_count), 0) == bucket_ref[...]
    bias = dot(table_ref[...].astype(BF16), onehot.astype(BF16))
    keys_ref[key_count:, :] = jnp.zeros((BIAS_ROWS, keys_ref.shape[1]), BF16)
    keys_ref[key_count:, :key_count] = (0.5 * bias).astype(BF16)


def cache_kernel(key_count, heads, keys_ref, w_ref, k_ref, v_ref):
    layers, width = w_ref.shape[0], w_ref.shape[1]
    head_size = width // heads
    normed = keys_ref[:key_count, :]
    bias = keys_ref[key_count:, :key_count]
    row = lax.broadcasted_iota(jnp.int32, (head_size, key_count), 0)
    for layer in range(layers):
        keys = silu(dot(w_ref[layer, :, :width], normed, TT)).astype(BF16)
        values = silu(dot(normed, w_ref[layer, :, width:])).astype(BF16)
        for head in range(heads):
            own = keys[head * head_size : (head + 1) * head_size]
            line = bias[layer * heads + head : layer * heads + head + 1].astype(F32)
            extra = jnp.where(row == 0, line, 0.0).astype(BF16)
            first, second = (own, extra) if head % 2 == 0 else (extra, own)
            k_ref[layer, head, :head_size, :] = first
            k_ref[layer, head, head_size:, :] = second
        for pair in range(heads // 2):
            v_ref[layer, pair] = values[:, pair * 128 : (pair + 1) * 128]


def layers_kernel(block, x_ref, k_ref, v_ref, wq_ref, wo_ref, out_ref, x_buf, q_buf, gate_buf, mixed_buf):
    rows, width = x_ref.shape
    layers, heads, pair_width, _ = k_ref.shape
    half = pair_width // 2
    scale = half**-0.5
    x_buf[...] = x_ref[...].astype(F32)
    for layer in range(layers):
        def project(step, _):
            at = pl.ds(pl.multiple_of(step * block, block), block)
            normed = layer_norm(x_buf[at, :]).astype(BF16)
            projected = silu(dot(normed, wq_ref[layer]))
            gate_buf[at, :] = projected[:, width:]
            queries = projected[:, :width].astype(BF16) * BF16(0.5 * scale)
            lane = lax.broadcasted_iota(jnp.int32, (block, pair_width), 1)
            for pair in range(heads // 2):
                own = queries[:, pair * pair_width : (pair + 1) * pair_width].astype(F32)
                q_buf[2 * pair, at, :] = jnp.where(lane < half, own, jnp.where(lane == half, 1.0, 0.0)).astype(BF16)
                q_buf[2 * pair + 1, at, :] = jnp.where(lane >= half, own, jnp.where(lane == 0, 1.0, 0.0)).astype(BF16)
            return 0

        lax.fori_loop(0, rows // block, project, 0)

        def attend(index, _):
            pair = index // (rows // block)
            at = pl.ds(pl.multiple_of((index % (rows // block)) * block, block), block)
            sums = []
            for side in range(2):
                scores = dot(q_buf[2 * pair + side, at, :], k_ref[layer, 2 * pair + side])
                sums.append(dot(silu_of_half(scores).astype(BF16), v_ref[layer, pair]))
            lane = lax.broadcasted_iota(jnp.int32, sums[0].shape, 1)
            mixed_buf[pair, at, :] = jnp.where(lane < half, sums[0], sums[1])
            return 0

        lax.fori_loop(0, heads // 2 * (rows // block), attend, 0)

        def finish(step, _):
            at = pl.ds(pl.multiple_of(step * block, block), block)
            mixed = jnp.concatenate([mixed_buf[pair, at, :] for pair in range(heads // 2)], axis=1)
            shaped = (layer_norm(mixed) * gate_buf[at, :]).astype(BF16)
            x_buf[at, :] = x_buf[at, :] + dot(shaped, wo_ref[layer])
            return 0

        lax.fori_loop(0, rows // block, finish, 0)
    out_ref[...] = x_buf[...].astype(BF16)


def rank_kernel(groups, capacity, back_ref, owner_ref, in_ref, w_out_ref, encoded_ref, logits_ref):
    rows = owner_ref.shape[0]
    slot_count = groups * capacity
    slot = slots_of(owner_ref[...], groups, capacity)
    place = (slot == lax.broadcasted_iota(jnp.int32, (rows, slot_count), 1)).astype(BF16)
    encoded = dot(place, back_ref[...]).astype(BF16)
    encoded_ref[...] = encoded
    normed = layer_norm(encoded.astype(F32)).astype(BF16)
    hidden = silu(dot(normed, in_ref[...])).astype(BF16)
    logits_ref[...] = dot(hidden, w_out_ref[...])


def params(mib):
    return pltpu.CompilerParams(vmem_limit_bytes=mib * MIB)


def shards(cand_feats, cand_user, history, hist_len, hist_bucket, w_qu, w_kv, w_out, bias_table, mlp_in, mlp_out):
    rows, width = cand_feats.shape
    groups, ctx = lax.axis_size("req"), lax.axis_size("ctx")
    capacity = 3 * rows // (2 * groups)
    slot_count = groups * capacity
    layers, heads, buckets = bias_table.shape
    key_count = history.shape[1]
    smem = pl.BlockSpec(memory_space=pltpu.SMEM)
    vmem = pl.BlockSpec(memory_space=pltpu.VMEM)
    outgoing, own_keys = pl.pallas_call(
        functools.partial(dispatch_kernel, groups, capacity),
        name="dispatch",
        in_specs=[smem] + [vmem] * 5,
        out_shape=(
            jax.ShapeDtypeStruct((slot_count, width), BF16),
            jax.ShapeDtypeStruct((key_count + BIAS_ROWS, width), BF16),
        ),
        compiler_params=params(32),
    )(hist_len, cand_feats, cand_user, history[0], hist_bucket, bias_table.reshape(layers * heads, buckets))

    block_rows = key_count + BIAS_ROWS
    same_core = [[i for i in range(ctx) if i % 2 == side] for side in range(2)]
    near = lax.all_to_all(
        jnp.broadcast_to(own_keys[None], (ctx // 2, block_rows, width)),
        "ctx", split_axis=0, concat_axis=0, tiled=True, axis_index_groups=same_core,
    )
    far = lax.ppermute(near, "ctx", [(i, i ^ 1) for i in range(ctx)])
    incoming = lax.all_to_all(
        outgoing.reshape(groups, capacity, width), "req", split_axis=0, concat_axis=0, tiled=True
    ).reshape(slot_count, width)

    all_keys = ctx * key_count
    blocks = jnp.concatenate([near, far], axis=0)
    cached_k, cached_v = pl.pallas_call(
        functools.partial(cache_kernel, key_count, heads),
        name="cache",
        grid=(ctx,),
        in_specs=[
            pl.BlockSpec((pl.Squeezed(), block_rows, width), lambda i: (i, 0, 0)),
            pl.BlockSpec((layers, width, 2 * width), lambda i: (0, 0, 0)),
        ],
        out_specs=(
            pl.BlockSpec((layers, heads, 128, key_count), lambda i: (0, 0, 0, i)),
            pl.BlockSpec((layers, heads // 2, key_count, 128), lambda i: (0, 0, i, 0)),
        ),
        out_shape=(
            jax.ShapeDtypeStruct((layers, heads, 128, all_keys), BF16),
            jax.ShapeDtypeStruct((layers, heads // 2, all_keys, 128), BF16),
        ),
        compiler_params=params(32),
    )(blocks, w_kv)
    finished = pl.pallas_call(
        functools.partial(layers_kernel, 256),
        name="layers",
        in_specs=[vmem] * 5,
        out_shape=jax.ShapeDtypeStruct((slot_count, width), BF16),
        scratch_shapes=[
            pltpu.VMEM((slot_count, width), F32),
            pltpu.VMEM((heads, slot_count, 128), BF16),
            pltpu.VMEM((slot_count, width), F32),
            pltpu.VMEM((heads // 2, slot_count, 128), F32),
        ],
        compiler_params=params(56),
    )(incoming, cached_k, cached_v, w_qu, w_out)
    returned = lax.all_to_all(
        finished.reshape(groups, capacity, width), "req", split_axis=0, concat_axis=0, tiled=True
    ).reshape(slot_count, width)
    return pl.pallas_call(
        functools.partial(rank_kernel, groups, capacity),
        name="rank",
        in_specs=[vmem] * 4,
        out_shape=(
            jax.ShapeDtypeStruct((rows, width), BF16),
            jax.ShapeDtypeStruct((rows, mlp_out.shape[1]), F32),
        ),
        compiler_params=params(32),
    )(returned, cand_user, mlp_in, mlp_out)


def solution(mesh):
    split = P(("req", "ctx"), None)
    in_specs = (split, split, P("req", "ctx", None), P(), P("req", "ctx"), P(), P(), P(), P(), P(), P())
    return jax.shard_map(shards, mesh=mesh, in_specs=in_specs, out_specs=(split, split), check_vma=False)
```

```python
import functools

import jax
import jax.numpy as jnp
from jax import lax
from jax.experimental import pallas as pl
from jax.experimental.pallas import tpu as pltpu
from jax.sharding import PartitionSpec as P

BF16 = jnp.bfloat16
F32 = jnp.float32
NT = (((1,), (1,)), ((), ()))
TN = (((0,), (0,)), ((), ()))
TT = (((0,), (1,)), ((), ()))
MIB = 2**20
BIAS_ROWS = 16


def dot(left, right, dims=(((1,), (0,)), ((), ()))):
    return lax.dot_general(left, right, dims, preferred_element_type=F32)


def layer_norm(values):
    average = jnp.mean(values, axis=-1, keepdims=True)
    centered = values - average
    spread = jnp.mean(centered * centered, axis=-1, keepdims=True)
    return centered * lax.rsqrt(spread + 1e-05)


def silu_of_half(half):
    return half + half * jnp.tanh(half)


def silu(values):
    return silu_of_half(0.5 * values)


def slots_of(owner_row, groups, capacity):
    rows = owner_row.shape[1]
    members = owner_row == lax.broadcasted_iota(jnp.int32, (groups, rows), 0)
    before = lax.broadcasted_iota(jnp.int32, (rows, rows), 0) < lax.broadcasted_iota(
        jnp.int32, (rows, rows), 1
    )
    earlier = dot(members.astype(BF16), before.astype(BF16))
    base = lax.broadcasted_iota(jnp.int32, (groups, rows), 0).astype(F32) * capacity
    return jnp.sum(jnp.where(members, earlier + base, 0.0), axis=0, keepdims=True)


def keys_kernel(len_ref, hist_ref, bucket_ref, table_ref, keys_ref):
    key_count = hist_ref.shape[0]
    live = len_ref[lax.axis_index("req")] - lax.axis_index("ctx") * key_count
    normed = layer_norm(hist_ref[...].astype(F32))
    position = lax.broadcasted_iota(jnp.int32, normed.shape, 0)
    keys_ref[:key_count, :] = jnp.where(position < live, normed, 0.0).astype(BF16)
    bucket_count = table_ref.shape[1]
    onehot = lax.broadcasted_iota(jnp.int32, (bucket_count, key_count), 0) == bucket_ref[...]
    bias = dot(table_ref[...].astype(BF16), onehot.astype(BF16))
    keys_ref[key_count:, :] = jnp.zeros((BIAS_ROWS, keys_ref.shape[1]), BF16)
    keys_ref[key_count:, :key_count] = (0.5 * bias).astype(BF16)


def dispatch_kernel(groups, capacity, feats_ref, owner_ref, out_ref):
    rows = feats_ref.shape[0]
    slot_count = groups * capacity
    slot = slots_of(owner_ref[...], groups, capacity).astype(jnp.int32)
    place = (slot == lax.broadcasted_iota(jnp.int32, (slot_count, rows), 0)).astype(BF16)
    out_ref[...] = dot(place, feats_ref[...]).astype(BF16)


def places_kernel(groups, capacity, owner_ref, place_ref):
    rows, slot_count = place_ref.shape
    slot = slots_of(owner_ref[...], groups, capacity)
    diagonal = lax.broadcasted_iota(jnp.int32, (rows, rows), 0) == lax.broadcasted_iota(
        jnp.int32, (rows, rows), 1
    )
    column = jnp.sum(jnp.where(diagonal, slot, 0.0), axis=1, keepdims=True).astype(jnp.int32)
    place_ref[...] = (column == lax.broadcasted_iota(jnp.int32, (rows, slot_count), 1)).astype(BF16)


def layers_kernel(heads, key_count, chunk_blocks, x_ref, *refs):
    blocks = refs[:chunk_blocks]
    wk_ref, wqu_ref, wo_ref, out_ref, x_buf, k_buf, b_buf, v_buf, q_buf, gate_buf, mixed_buf = refs[chunk_blocks:]
    rows, width = x_ref.shape
    layers = wk_ref.shape[0]
    half = width // heads
    pairs = heads // 2
    scale = BF16(0.5 * half**-0.5)

    pieces = [(ref, i) for ref in blocks for i in range(ref.shape[0])]
    per = 4
    eye = (
        lax.broadcasted_iota(jnp.int32, (BIAS_ROWS, 128), 0) == lax.broadcasted_iota(jnp.int32, (BIAS_ROWS, 128), 1)
    ).astype(BF16)
    for first in range(0, len(pieces), per):
        group = pieces[first : first + per]
        at = slice(first * key_count, (first + per) * key_count)
        normed = jnp.concatenate([ref[i, :key_count, :] for ref, i in group], axis=0)
        bias = jnp.concatenate([ref[i, key_count:, :key_count] for ref, i in group], axis=1)
        b_buf[at, :] = dot(bias, eye, TN).astype(BF16)
        for layer in range(layers):
            keys = silu(dot(normed, wk_ref[layer, :, :width])).astype(BF16)
            for pair in range(pairs):
                k_buf[layer, pair, at, :] = keys[:, pair * 128 : (pair + 1) * 128]
            v_buf[layer, :, at] = silu(dot(wk_ref[layer, :, width:], normed, TT)).astype(BF16)

    x_buf[...] = x_ref[...].astype(F32)
    for layer in range(layers):
        normed = layer_norm(x_buf[...]).astype(BF16)
        for part in range(0, 2 * width, 256):
            projected = silu(dot(wqu_ref[layer, :, part : part + 256], normed, TT))
            if part < width:
                q_buf[part : part + 256, :] = projected.astype(BF16) * scale
            else:
                gate_buf[part - width : part - width + 256, :] = projected

        def attend(pair, _):
            bias = b_buf[...]
            left = jnp.concatenate([k_buf[layer, pair], bias], axis=1)
            for side in range(2):
                head = 2 * pair + side
                own = q_buf[pl.ds(pl.multiple_of(head * half, half), half), :]
                none = jnp.zeros((half, rows), BF16)
                row = lax.broadcasted_iota(jnp.int32, (128, rows), 0)
                pick = (row == layer * heads + head).astype(BF16)
                right = jnp.concatenate([own, none, pick] if side == 0 else [none, own, pick], axis=0)
                weights = silu_of_half(dot(left, right)).astype(BF16)
                at = pl.ds(pl.multiple_of(head * half, half), half)
                mixed_buf[at, :] = dot(v_buf[layer, at, :], weights)
            return 0

        lax.fori_loop(0, pairs, attend, 0)
        mixed = mixed_buf[...]
        centered = mixed - jnp.mean(mixed, axis=0, keepdims=True)
        spread = jnp.mean(centered * centered, axis=0, keepdims=True)
        shaped = (centered * lax.rsqrt(spread + 1e-05) * gate_buf[...]).astype(BF16)
        x_buf[...] = x_buf[...] + dot(shaped, wo_ref[layer], TN)
    out_ref[...] = x_buf[...].astype(BF16)


def rank_kernel(back_ref, place_ref, in_ref, w_out_ref, encoded_ref, logits_ref):
    encoded = dot(place_ref[...], back_ref[...]).astype(BF16)
    encoded_ref[...] = encoded
    normed = layer_norm(encoded.astype(F32)).astype(BF16)
    hidden = silu(dot(normed, in_ref[...])).astype(BF16)
    logits_ref[...] = dot(w_out_ref[...], hidden, NT)


def whole(*shape):
    return pl.BlockSpec(shape, lambda i: (0,) * len(shape))


def params(mib):
    return pltpu.CompilerParams(vmem_limit_bytes=mib * MIB)


def shards(cand_feats, cand_user, history, hist_len, hist_bucket, w_qu, w_kv, w_out, bias_table, mlp_in, mlp_out):
    rows, width = cand_feats.shape
    groups, ctx = lax.axis_size("req"), lax.axis_size("ctx")
    capacity = 3 * rows // (2 * groups)
    slot_count = groups * capacity
    layers, heads, buckets = bias_table.shape
    key_count = history.shape[1]
    smem = pl.BlockSpec(memory_space=pltpu.SMEM)
    vmem = pl.BlockSpec(memory_space=pltpu.VMEM)
    owners = cand_user.reshape(1, rows)
    own_keys = pl.pallas_call(
        keys_kernel,
        name="keys",
        grid=(1,),
        in_specs=[smem, whole(key_count, width), whole(1, key_count), whole(layers * heads, buckets)],
        out_specs=whole(key_count + BIAS_ROWS, width),
        out_shape=jax.ShapeDtypeStruct((key_count + BIAS_ROWS, width), BF16),
        compiler_params=params(60),
    )(hist_len, history[0], hist_bucket, bias_table.reshape(layers * heads, buckets))
    block_rows = key_count + BIAS_ROWS

    def hop(array, dy, dz, dc):
        places = [(y, z, c) for y in range(2) for z in range(ctx // 4) for c in range(2)]
        index = {place: i for i, place in enumerate(places)}
        pairs = [
            (index[y, z, c], index[(y + dy) % 2, (z + dz) % (ctx // 4), (c + dc) % 2]) for y, z, c in places
        ]
        return lax.ppermute(array, "ctx", pairs)

    across = hop(own_keys, 1, 0, 0)
    outgoing = pl.pallas_call(
        functools.partial(dispatch_kernel, groups, capacity),
        name="dispatch",
        grid=(1,),
        in_specs=[whole(rows, width), whole(1, rows)],
        out_specs=whole(slot_count, width),
        out_shape=jax.ShapeDtypeStruct((slot_count, width), BF16),
        compiler_params=params(60),
    )(cand_feats, owners)
    own_keys, outgoing = lax.optimization_barrier((own_keys, outgoing))
    near = jnp.stack([own_keys] + [hop(own_keys, 0, step, 0) for step in (1, 3, 2)])
    incoming = lax.all_to_all(
        outgoing.reshape(groups, capacity, width), "req", split_axis=0, concat_axis=0, tiled=True
    ).reshape(slot_count, width)
    far = jnp.stack([across] + [hop(across, 0, step, 0) for step in (1, 3, 2)])
    blocks = [near, hop(near, 0, 0, 1), far, hop(far, 0, 0, 1)]

    all_keys = ctx * key_count
    finished = pl.pallas_call(
        functools.partial(layers_kernel, heads, key_count, len(blocks)),
        name="layers",
        in_specs=[vmem] * (4 + len(blocks)),
        out_shape=jax.ShapeDtypeStruct((slot_count, width), BF16),
        scratch_shapes=[
            pltpu.VMEM((slot_count, width), F32),
            pltpu.VMEM((layers, heads // 2, all_keys, 128), BF16),
            pltpu.VMEM((all_keys, 128), BF16),
            pltpu.VMEM((layers, width, all_keys), BF16),
            pltpu.VMEM((width, slot_count), BF16),
            pltpu.VMEM((width, slot_count), F32),
            pltpu.VMEM((width, slot_count), F32),
        ],
        compiler_params=params(56),
    )(
        incoming,
        *blocks,
        w_kv,
        w_qu,
        w_out,
    )
    returned = lax.all_to_all(
        finished.reshape(groups, capacity, width), "req", split_axis=0, concat_axis=0, tiled=True
    ).reshape(slot_count, width)
    place = pl.pallas_call(
        functools.partial(places_kernel, groups, capacity),
        name="places",
        grid=(1,),
        in_specs=[whole(1, rows)],
        out_specs=whole(rows, slot_count),
        out_shape=jax.ShapeDtypeStruct((rows, slot_count), BF16),
        compiler_params=params(16),
    )(owners)
    tasks = mlp_out.shape[1]
    encoded, logits = pl.pallas_call(
        rank_kernel,
        name="rank",
        in_specs=[vmem] * 4,
        out_shape=(
            jax.ShapeDtypeStruct((rows, width), BF16),
            jax.ShapeDtypeStruct((tasks, rows), F32),
        ),
        compiler_params=params(16),
    )(returned, place, mlp_in, mlp_out.T)
    return encoded, logits.T


def solution(mesh):
    split = P(("req", "ctx"), None)
    in_specs = (split, split, P("req", "ctx", None), P(), P("req", "ctx"), P(), P(), P(), P(), P(), P())
    return jax.shard_map(shards, mesh=mesh, in_specs=in_specs, out_specs=(split, split), check_vma=False)
```

```python
import functools

import jax
import jax.numpy as jnp
from jax import lax
from jax.experimental import pallas as pl
from jax.experimental.pallas import tpu as pltpu
from jax.sharding import PartitionSpec as P

BF16 = jnp.bfloat16
F32 = jnp.float32
NT = (((1,), (1,)), ((), ()))
TN = (((0,), (0,)), ((), ()))
TT = (((0,), (1,)), ((), ()))
MIB = 2**20
BIAS_ROWS = 16


def dot(left, right, dims=(((1,), (0,)), ((), ()))):
    return lax.dot_general(left, right, dims, preferred_element_type=F32)


def layer_norm(values):
    average = jnp.mean(values, axis=-1, keepdims=True)
    centered = values - average
    spread = jnp.mean(centered * centered, axis=-1, keepdims=True)
    return centered * lax.rsqrt(spread + 1e-05)


def silu_of_half(half):
    return half + half * jnp.tanh(half)


def silu(values):
    return silu_of_half(0.5 * values)


def slots_of(owner_row, groups, capacity):
    rows = owner_row.shape[1]
    members = owner_row == lax.broadcasted_iota(jnp.int32, (groups, rows), 0)
    before = lax.broadcasted_iota(jnp.int32, (rows, rows), 0) < lax.broadcasted_iota(
        jnp.int32, (rows, rows), 1
    )
    earlier = dot(members.astype(BF16), before.astype(BF16))
    base = lax.broadcasted_iota(jnp.int32, (groups, rows), 0).astype(F32) * capacity
    return jnp.sum(jnp.where(members, earlier + base, 0.0), axis=0, keepdims=True)


def keys_kernel(len_ref, hist_ref, bucket_ref, table_ref, keys_ref):
    key_count = hist_ref.shape[0]
    live = len_ref[lax.axis_index("req")] - lax.axis_index("ctx") * key_count
    normed = layer_norm(hist_ref[...].astype(F32))
    position = lax.broadcasted_iota(jnp.int32, normed.shape, 0)
    keys_ref[:key_count, :] = jnp.where(position < live, normed, 0.0).astype(BF16)
    bucket_count = table_ref.shape[1]
    onehot = lax.broadcasted_iota(jnp.int32, (bucket_count, key_count), 0) == bucket_ref[...]
    bias = dot(table_ref[...].astype(BF16), onehot.astype(BF16))
    keys_ref[key_count:, :] = jnp.zeros((BIAS_ROWS, keys_ref.shape[1]), BF16)
    keys_ref[key_count:, :key_count] = (0.5 * bias).astype(BF16)


def dispatch_kernel(groups, capacity, feats_ref, owner_ref, out_ref):
    rows = feats_ref.shape[0]
    slot_count = groups * capacity
    slot = slots_of(owner_ref[...], groups, capacity).astype(jnp.int32)
    place = (slot == lax.broadcasted_iota(jnp.int32, (slot_count, rows), 0)).astype(BF16)
    out_ref[...] = dot(place, feats_ref[...]).astype(BF16)


def places_kernel(groups, capacity, owner_ref, place_ref):
    rows, slot_count = place_ref.shape
    slot = slots_of(owner_ref[...], groups, capacity)
    diagonal = lax.broadcasted_iota(jnp.int32, (rows, rows), 0) == lax.broadcasted_iota(
        jnp.int32, (rows, rows), 1
    )
    column = jnp.sum(jnp.where(diagonal, slot, 0.0), axis=1, keepdims=True).astype(jnp.int32)
    place_ref[...] = (column == lax.broadcasted_iota(jnp.int32, (rows, slot_count), 1)).astype(BF16)


def layers_kernel(heads, key_count, chunk_blocks, x_hbm, *refs):
    blocks_hbm = refs[:chunk_blocks]
    wk_hbm, wqu_hbm, wo_hbm, out_ref, x_buf, k_buf, b_buf, v_buf, q_buf, gate_buf, mixed_buf = refs[chunk_blocks:-6]
    x_ref, blocks, wk_ref, wqu_ref, wo_ref, sems = refs[-6:]
    rows, width = x_ref.shape
    layers = wk_ref.shape[0]

    block_copies = [
        pltpu.make_async_copy(blocks_hbm[i], blocks.at[i], sems.at[i]) for i in range(chunk_blocks)
    ]
    wk_copies = [
        pltpu.make_async_copy(wk_hbm.at[layer], wk_ref.at[layer], sems.at[chunk_blocks + layer])
        for layer in range(layers)
    ]
    x_copy = pltpu.make_async_copy(x_hbm, x_ref, sems.at[chunk_blocks + layers])
    wqu_copy = pltpu.make_async_copy(wqu_hbm, wqu_ref, sems.at[chunk_blocks + layers + 1])
    wo_copy = pltpu.make_async_copy(wo_hbm, wo_ref, sems.at[chunk_blocks + layers + 2])
    for copy in [block_copies[0], *wk_copies, *block_copies[1:], x_copy, wqu_copy, wo_copy]:
        copy.start()
    half = width // heads
    pairs = heads // 2
    scale = BF16(0.5 * half**-0.5)

    per = blocks.shape[1]
    eye = (
        lax.broadcasted_iota(jnp.int32, (BIAS_ROWS, 128), 0) == lax.broadcasted_iota(jnp.int32, (BIAS_ROWS, 128), 1)
    ).astype(BF16)
    for group in range(chunk_blocks):
        at = slice(group * per * key_count, (group + 1) * per * key_count)
        block_copies[group].wait()
        normed = jnp.concatenate([blocks[group, i, :key_count, :] for i in range(per)], axis=0)
        bias = jnp.concatenate([blocks[group, i, key_count:, :key_count] for i in range(per)], axis=1)
        b_buf[at, :] = dot(bias, eye, TN).astype(BF16)
        for layer in range(layers):
            if group == 0:
                wk_copies[layer].wait()
            keys = silu(dot(normed, wk_ref[layer, :, :width])).astype(BF16)
            for pair in range(pairs):
                k_buf[layer, pair, at, :] = keys[:, pair * 128 : (pair + 1) * 128]
            v_buf[layer, :, at] = silu(dot(wk_ref[layer, :, width:], normed, TT)).astype(BF16)

    x_copy.wait()
    wqu_copy.wait()
    wo_copy.wait()
    x_buf[...] = x_ref[...].astype(F32)
    for layer in range(layers):
        normed = layer_norm(x_buf[...]).astype(BF16)
        for part in range(0, 2 * width, 256):
            projected = silu(dot(wqu_ref[layer, :, part : part + 256], normed, TT))
            if part < width:
                q_buf[part : part + 256, :] = projected.astype(BF16) * scale
            else:
                gate_buf[part - width : part - width + 256, :] = projected

        def attend(pair, _):
            bias = b_buf[...]
            left = jnp.concatenate([k_buf[layer, pair], bias], axis=1)
            for side in range(2):
                head = 2 * pair + side
                own = q_buf[pl.ds(pl.multiple_of(head * half, half), half), :]
                none = jnp.zeros((half, rows), BF16)
                row = lax.broadcasted_iota(jnp.int32, (128, rows), 0)
                pick = (row == layer * heads + head).astype(BF16)
                right = jnp.concatenate([own, none, pick] if side == 0 else [none, own, pick], axis=0)
                weights = silu_of_half(dot(left, right)).astype(BF16)
                at = pl.ds(pl.multiple_of(head * half, half), half)
                mixed_buf[at, :] = dot(v_buf[layer, at, :], weights)
            return 0

        lax.fori_loop(0, pairs, attend, 0)
        mixed = mixed_buf[...]
        centered = mixed - jnp.mean(mixed, axis=0, keepdims=True)
        spread = jnp.mean(centered * centered, axis=0, keepdims=True)
        shaped = (centered * lax.rsqrt(spread + 1e-05) * gate_buf[...]).astype(BF16)
        x_buf[...] = x_buf[...] + dot(shaped, wo_ref[layer], TN)
    out_ref[...] = x_buf[...].astype(BF16)


def rank_kernel(back_ref, place_ref, in_ref, w_out_ref, encoded_ref, logits_ref):
    encoded = dot(place_ref[...], back_ref[...]).astype(BF16)
    encoded_ref[...] = encoded
    normed = layer_norm(encoded.astype(F32)).astype(BF16)
    hidden = silu(dot(normed, in_ref[...])).astype(BF16)
    logits_ref[...] = dot(w_out_ref[...], hidden, NT)


def whole(*shape):
    return pl.BlockSpec(shape, lambda i: (0,) * len(shape))


def params(mib):
    return pltpu.CompilerParams(vmem_limit_bytes=mib * MIB)


def shards(cand_feats, cand_user, history, hist_len, hist_bucket, w_qu, w_kv, w_out, bias_table, mlp_in, mlp_out):
    rows, width = cand_feats.shape
    groups, ctx = lax.axis_size("req"), lax.axis_size("ctx")
    capacity = 3 * rows // (2 * groups)
    slot_count = groups * capacity
    layers, heads, buckets = bias_table.shape
    key_count = history.shape[1]
    smem = pl.BlockSpec(memory_space=pltpu.SMEM)
    vmem = pl.BlockSpec(memory_space=pltpu.VMEM)
    owners = cand_user.reshape(1, rows)
    own_keys = pl.pallas_call(
        keys_kernel,
        name="keys",
        grid=(1,),
        in_specs=[smem, whole(key_count, width), whole(1, key_count), whole(layers * heads, buckets)],
        out_specs=whole(key_count + BIAS_ROWS, width),
        out_shape=jax.ShapeDtypeStruct((key_count + BIAS_ROWS, width), BF16),
        compiler_params=params(60),
    )(hist_len, history[0], hist_bucket, bias_table.reshape(layers * heads, buckets))
    block_rows = key_count + BIAS_ROWS

    def hop(array, dy, dz, dc):
        places = [(y, z, c) for y in range(2) for z in range(ctx // 4) for c in range(2)]
        index = {place: i for i, place in enumerate(places)}
        pairs = [
            (index[y, z, c], index[(y + dy) % 2, (z + dz) % (ctx // 4), (c + dc) % 2]) for y, z, c in places
        ]
        return lax.ppermute(array, "ctx", pairs)

    across = hop(own_keys, 1, 0, 0)
    outgoing = pl.pallas_call(
        functools.partial(dispatch_kernel, groups, capacity),
        name="dispatch",
        grid=(1,),
        in_specs=[whole(rows, width), whole(1, rows)],
        out_specs=whole(slot_count, width),
        out_shape=jax.ShapeDtypeStruct((slot_count, width), BF16),
        compiler_params=params(60),
    )(cand_feats, owners)
    own_keys, outgoing = lax.optimization_barrier((own_keys, outgoing))
    near = jnp.stack([own_keys] + [hop(own_keys, 0, step, 0) for step in (1, 3, 2)])
    incoming = lax.all_to_all(
        outgoing.reshape(groups, capacity, width), "req", split_axis=0, concat_axis=0, tiled=True
    ).reshape(slot_count, width)
    far = jnp.stack([across] + [hop(across, 0, step, 0) for step in (1, 3, 2)])
    blocks = [near, hop(near, 0, 0, 1), far, hop(far, 0, 0, 1)]

    all_keys = ctx * key_count
    finished = pl.pallas_call(
        functools.partial(layers_kernel, heads, key_count, len(blocks)),
        name="layers",
        in_specs=[pl.BlockSpec(memory_space=pl.ANY)] * (4 + len(blocks)),
        out_shape=jax.ShapeDtypeStruct((slot_count, width), BF16),
        scratch_shapes=[
            pltpu.VMEM((slot_count, width), F32),
            pltpu.VMEM((layers, heads // 2, all_keys, 128), BF16),
            pltpu.VMEM((all_keys, 128), BF16),
            pltpu.VMEM((layers, width, all_keys), BF16),
            pltpu.VMEM((width, slot_count), BF16),
            pltpu.VMEM((width, slot_count), F32),
            pltpu.VMEM((width, slot_count), F32),
            pltpu.VMEM((slot_count, width), BF16),
            pltpu.VMEM((len(blocks), *blocks[0].shape), BF16),
            pltpu.VMEM(w_kv.shape, BF16),
            pltpu.VMEM(w_qu.shape, BF16),
            pltpu.VMEM(w_out.shape, BF16),
            pltpu.SemaphoreType.DMA((len(blocks) + layers + 3,)),
        ],
        compiler_params=params(56),
    )(
        incoming,
        *blocks,
        w_kv,
        w_qu,
        w_out,
    )
    returned = lax.all_to_all(
        finished.reshape(groups, capacity, width), "req", split_axis=0, concat_axis=0, tiled=True
    ).reshape(slot_count, width)
    place = pl.pallas_call(
        functools.partial(places_kernel, groups, capacity),
        name="places",
        grid=(1,),
        in_specs=[whole(1, rows)],
        out_specs=whole(rows, slot_count),
        out_shape=jax.ShapeDtypeStruct((rows, slot_count), BF16),
        compiler_params=params(16),
    )(owners)
    tasks = mlp_out.shape[1]
    encoded, logits = pl.pallas_call(
        rank_kernel,
        name="rank",
        in_specs=[vmem] * 4,
        out_shape=(
            jax.ShapeDtypeStruct((rows, width), BF16),
            jax.ShapeDtypeStruct((tasks, rows), F32),
        ),
        compiler_params=params(16),
    )(returned, place, mlp_in, mlp_out.T)
    return encoded, logits.T


def solution(mesh):
    split = P(("req", "ctx"), None)
    in_specs = (split, split, P("req", "ctx", None), P(), P("req", "ctx"), P(), P(), P(), P(), P(), P())
    return jax.shard_map(shards, mesh=mesh, in_specs=in_specs, out_specs=(split, split), check_vma=False)
```

```python
import functools

import jax
import jax.numpy as jnp
from jax import lax
from jax.experimental import pallas as pl
from jax.experimental.pallas import tpu as pltpu
from jax.sharding import PartitionSpec as P

BF16 = jnp.bfloat16
F32 = jnp.float32
NT = (((1,), (1,)), ((), ()))
TN = (((0,), (0,)), ((), ()))
TT = (((0,), (1,)), ((), ()))
MIB = 2**20
BIAS_ROWS = 16


def dot(left, right, dims=(((1,), (0,)), ((), ()))):
    return lax.dot_general(left, right, dims, preferred_element_type=F32)


def layer_norm(values):
    average = jnp.mean(values, axis=-1, keepdims=True)
    centered = values - average
    spread = jnp.mean(centered * centered, axis=-1, keepdims=True)
    return centered * lax.rsqrt(spread + 1e-05)


def silu_of_half(half):
    return half + half * jnp.tanh(half)


def silu(values):
    return silu_of_half(0.5 * values)


def slots_of(owner_row, groups, capacity):
    rows = owner_row.shape[1]
    members = owner_row == lax.broadcasted_iota(jnp.int32, (groups, rows), 0)
    before = lax.broadcasted_iota(jnp.int32, (rows, rows), 0) < lax.broadcasted_iota(
        jnp.int32, (rows, rows), 1
    )
    earlier = dot(members.astype(BF16), before.astype(BF16))
    base = lax.broadcasted_iota(jnp.int32, (groups, rows), 0).astype(F32) * capacity
    return jnp.sum(jnp.where(members, earlier + base, 0.0), axis=0, keepdims=True)


def keys_kernel(len_ref, hist_ref, bucket_ref, table_ref, keys_ref):
    key_count = hist_ref.shape[0]
    live = len_ref[lax.axis_index("req")] - lax.axis_index("ctx") * key_count
    normed = layer_norm(hist_ref[...].astype(F32))
    position = lax.broadcasted_iota(jnp.int32, normed.shape, 0)
    keys_ref[:key_count, :] = jnp.where(position < live, normed, 0.0).astype(BF16)
    bucket_count = table_ref.shape[1]
    onehot = lax.broadcasted_iota(jnp.int32, (bucket_count, key_count), 0) == bucket_ref[...]
    bias = dot(table_ref[...].astype(BF16), onehot.astype(BF16))
    keys_ref[key_count:, :] = jnp.zeros((BIAS_ROWS, keys_ref.shape[1]), BF16)
    keys_ref[key_count:, :key_count] = (0.5 * bias).astype(BF16)


def dispatch_kernel(groups, capacity, feats_ref, owner_ref, out_ref):
    rows = feats_ref.shape[0]
    slot_count = groups * capacity
    slot = slots_of(owner_ref[...], groups, capacity).astype(jnp.int32)
    place = (slot == lax.broadcasted_iota(jnp.int32, (slot_count, rows), 0)).astype(BF16)
    out_ref[...] = dot(place, feats_ref[...]).astype(BF16)


def places_kernel(groups, capacity, owner_ref, place_ref):
    rows, slot_count = place_ref.shape
    slot = slots_of(owner_ref[...], groups, capacity)
    diagonal = lax.broadcasted_iota(jnp.int32, (rows, rows), 0) == lax.broadcasted_iota(
        jnp.int32, (rows, rows), 1
    )
    column = jnp.sum(jnp.where(diagonal, slot, 0.0), axis=1, keepdims=True).astype(jnp.int32)
    place_ref[...] = (column == lax.broadcasted_iota(jnp.int32, (rows, slot_count), 1)).astype(BF16)


def layers_kernel(heads, key_count, chunk_blocks, x_hbm, *refs):
    blocks_hbm = refs[:chunk_blocks]
    wk_hbm, wqu_hbm, wo_hbm, out_hbm, x_buf, k_buf, b_buf, v_buf, q_buf, gate_buf, mixed_buf = refs[chunk_blocks:-6]
    x_ref, blocks, wk_ref, wqu_ref, wo_ref, sems = refs[-6:]
    rows, width = x_ref.shape
    layers = wk_ref.shape[0]

    block_copies = [
        pltpu.make_async_copy(blocks_hbm[i], blocks.at[i], sems.at[i]) for i in range(chunk_blocks)
    ]
    wk_copies = [
        pltpu.make_async_copy(wk_hbm.at[layer], wk_ref.at[layer], sems.at[chunk_blocks + layer])
        for layer in range(layers)
    ]
    x_copy = pltpu.make_async_copy(x_hbm, x_ref, sems.at[chunk_blocks + layers])
    wqu_copy = pltpu.make_async_copy(wqu_hbm, wqu_ref, sems.at[chunk_blocks + layers + 1])
    wo_copy = pltpu.make_async_copy(wo_hbm, wo_ref, sems.at[chunk_blocks + layers + 2])
    for copy in [*block_copies[:2], *wk_copies, *block_copies[2:], x_copy, wqu_copy, wo_copy]:
        copy.start()
    half = width // heads
    pairs = heads // 2
    scale = BF16(0.5 * half**-0.5)

    per = blocks.shape[1]
    eye = (
        lax.broadcasted_iota(jnp.int32, (BIAS_ROWS, 128), 0) == lax.broadcasted_iota(jnp.int32, (BIAS_ROWS, 128), 1)
    ).astype(BF16)
    for group in range(0, chunk_blocks, 2):
        at = slice(group * per * key_count, (group + 2) * per * key_count)
        pieces = [(group + side, i) for side in range(2) for i in range(per)]
        for side in range(2):
            block_copies[group + side].wait()
        normed = jnp.concatenate([blocks[g, i, :key_count, :] for g, i in pieces], axis=0)
        bias = jnp.concatenate([blocks[g, i, key_count:, :key_count] for g, i in pieces], axis=1)
        b_buf[at, :] = dot(bias, eye, TN).astype(BF16)
        for layer in range(layers):
            if group == 0:
                wk_copies[layer].wait()
            keys = silu(dot(normed, wk_ref[layer, :, :width])).astype(BF16)
            for pair in range(pairs):
                k_buf[layer, pair, at, :] = keys[:, pair * 128 : (pair + 1) * 128]
            v_buf[layer, :, at] = silu(dot(wk_ref[layer, :, width:], normed, TT)).astype(BF16)

    x_copy.wait()
    wqu_copy.wait()
    wo_copy.wait()
    x_buf[...] = x_ref[...].astype(F32)
    for layer in range(layers):
        normed = layer_norm(x_buf[...]).astype(BF16)
        for part in range(0, 2 * width, 256):
            projected = silu(dot(wqu_ref[layer, :, part : part + 256], normed, TT))
            if part < width:
                q_buf[part : part + 256, :] = projected.astype(BF16) * scale
            else:
                gate_buf[part - width : part - width + 256, :] = projected

        def attend(pair, _):
            bias = b_buf[...]
            left = jnp.concatenate([k_buf[layer, pair], bias], axis=1)
            for side in range(2):
                head = 2 * pair + side
                own = q_buf[pl.ds(pl.multiple_of(head * half, half), half), :]
                none = jnp.zeros((half, rows), BF16)
                row = lax.broadcasted_iota(jnp.int32, (128, rows), 0)
                pick = (row == layer * heads + head).astype(BF16)
                right = jnp.concatenate([own, none, pick] if side == 0 else [none, own, pick], axis=0)
                weights = silu_of_half(dot(left, right)).astype(BF16)
                at = pl.ds(pl.multiple_of(head * half, half), half)
                mixed_buf[at, :] = dot(v_buf[layer, at, :], weights)
            return 0

        lax.fori_loop(0, pairs, attend, 0)
        mixed = mixed_buf[...]
        centered = mixed - jnp.mean(mixed, axis=0, keepdims=True)
        spread = jnp.mean(centered * centered, axis=0, keepdims=True)
        shaped = (centered * lax.rsqrt(spread + 1e-05) * gate_buf[...]).astype(BF16)
        if layer + 1 < layers:
            x_buf[...] = x_buf[...] + dot(shaped, wo_ref[layer], TN)
    part = 256
    out_copies = []
    for first in range(0, rows, part):
        at = slice(first, first + part)
        x_ref[at, :] = (x_buf[at, :] + dot(shaped[:, at], wo_ref[layers - 1], TN)).astype(BF16)
        out_copies.append(pltpu.make_async_copy(x_ref.at[at, :], out_hbm.at[at, :], sems.at[first // part]))
        out_copies[-1].start()
    for copy in out_copies:
        copy.wait()


def rank_kernel(back_ref, place_ref, in_ref, w_out_ref, encoded_ref, logits_ref):
    encoded = dot(place_ref[...], back_ref[...]).astype(BF16)
    encoded_ref[...] = encoded
    normed = layer_norm(encoded.astype(F32)).astype(BF16)
    hidden = silu(dot(normed, in_ref[...])).astype(BF16)
    logits_ref[...] = dot(w_out_ref[...], hidden, NT)


def whole(*shape):
    return pl.BlockSpec(shape, lambda i: (0,) * len(shape))


def params(mib):
    return pltpu.CompilerParams(vmem_limit_bytes=mib * MIB)


def shards(cand_feats, cand_user, history, hist_len, hist_bucket, w_qu, w_kv, w_out, bias_table, mlp_in, mlp_out):
    rows, width = cand_feats.shape
    groups, ctx = lax.axis_size("req"), lax.axis_size("ctx")
    capacity = 3 * rows // (2 * groups)
    slot_count = groups * capacity
    layers, heads, buckets = bias_table.shape
    key_count = history.shape[1]
    smem = pl.BlockSpec(memory_space=pltpu.SMEM)
    vmem = pl.BlockSpec(memory_space=pltpu.VMEM)
    owners = cand_user.reshape(1, rows)
    own_keys = pl.pallas_call(
        keys_kernel,
        name="keys",
        grid=(1,),
        in_specs=[smem, whole(key_count, width), whole(1, key_count), whole(layers * heads, buckets)],
        out_specs=whole(key_count + BIAS_ROWS, width),
        out_shape=jax.ShapeDtypeStruct((key_count + BIAS_ROWS, width), BF16),
        compiler_params=params(60),
    )(hist_len, history[0], hist_bucket, bias_table.reshape(layers * heads, buckets))
    block_rows = key_count + BIAS_ROWS

    def hop(array, dy, dz, dc):
        places = [(y, z, c) for y in range(2) for z in range(ctx // 4) for c in range(2)]
        index = {place: i for i, place in enumerate(places)}
        pairs = [
            (index[y, z, c], index[(y + dy) % 2, (z + dz) % (ctx // 4), (c + dc) % 2]) for y, z, c in places
        ]
        return lax.ppermute(array, "ctx", pairs)

    across = hop(own_keys, 1, 0, 0)
    outgoing = pl.pallas_call(
        functools.partial(dispatch_kernel, groups, capacity),
        name="dispatch",
        grid=(1,),
        in_specs=[whole(rows, width), whole(1, rows)],
        out_specs=whole(slot_count, width),
        out_shape=jax.ShapeDtypeStruct((slot_count, width), BF16),
        compiler_params=params(60),
    )(cand_feats, owners)
    own_keys, outgoing = lax.optimization_barrier((own_keys, outgoing))
    near = jnp.stack([own_keys] + [hop(own_keys, 0, step, 0) for step in (1, 3, 2)])
    incoming = lax.all_to_all(
        outgoing.reshape(groups, capacity, width), "req", split_axis=0, concat_axis=0, tiled=True
    ).reshape(slot_count, width)
    far = jnp.stack([across] + [hop(across, 0, step, 0) for step in (1, 3, 2)])
    blocks = [near, hop(near, 0, 0, 1), far, hop(far, 0, 0, 1)]

    all_keys = ctx * key_count
    finished = pl.pallas_call(
        functools.partial(layers_kernel, heads, key_count, len(blocks)),
        name="layers",
        in_specs=[pl.BlockSpec(memory_space=pl.ANY)] * (4 + len(blocks)),
        out_specs=pl.BlockSpec(memory_space=pl.ANY),
        out_shape=jax.ShapeDtypeStruct((slot_count, width), BF16),
        scratch_shapes=[
            pltpu.VMEM((slot_count, width), F32),
            pltpu.VMEM((layers, heads // 2, all_keys, 128), BF16),
            pltpu.VMEM((all_keys, 128), BF16),
            pltpu.VMEM((layers, width, all_keys), BF16),
            pltpu.VMEM((width, slot_count), BF16),
            pltpu.VMEM((width, slot_count), F32),
            pltpu.VMEM((width, slot_count), F32),
            pltpu.VMEM((slot_count, width), BF16),
            pltpu.VMEM((len(blocks), *blocks[0].shape), BF16),
            pltpu.VMEM(w_kv.shape, BF16),
            pltpu.VMEM(w_qu.shape, BF16),
            pltpu.VMEM(w_out.shape, BF16),
            pltpu.SemaphoreType.DMA((len(blocks) + layers + 3,)),
        ],
        compiler_params=params(56),
    )(
        incoming,
        *blocks,
        w_kv,
        w_qu,
        w_out,
    )
    returned = lax.all_to_all(
        finished.reshape(groups, capacity, width), "req", split_axis=0, concat_axis=0, tiled=True
    ).reshape(slot_count, width)
    place = pl.pallas_call(
        functools.partial(places_kernel, groups, capacity),
        name="places",
        grid=(1,),
        in_specs=[whole(1, rows)],
        out_specs=whole(rows, slot_count),
        out_shape=jax.ShapeDtypeStruct((rows, slot_count), BF16),
        compiler_params=params(16),
    )(owners)
    tasks = mlp_out.shape[1]
    encoded, logits = pl.pallas_call(
        rank_kernel,
        name="rank",
        in_specs=[vmem] * 4,
        out_shape=(
            jax.ShapeDtypeStruct((rows, width), BF16),
            jax.ShapeDtypeStruct((tasks, rows), F32),
        ),
        compiler_params=params(16),
    )(returned, place, mlp_in, mlp_out.T)
    return encoded, logits.T


def solution(mesh):
    split = P(("req", "ctx"), None)
    in_specs = (split, split, P("req", "ctx", None), P(), P("req", "ctx"), P(), P(), P(), P(), P(), P())
    return jax.shard_map(shards, mesh=mesh, in_specs=in_specs, out_specs=(split, split), check_vma=False)
```
